256 devices in a mesh: seq: 128 (over z, y, x_lo, core), cfg: 2 (over x_hi).
Axes of the slice: x: 4 (x_hi: 2, x_lo: 2; x = x_hi * 2 + x_lo), y: 4, z: 8, core: 2. Of those that a mesh axis runs over, the one named last changes fastest.
Arguments:
- queries: bfloat16 [65536, 2560], P(('cfg', 'seq')), parts along dimension 0, may hold values from -40 to 40
- latent_keys: bfloat16 [65536, 2560], P(('cfg', 'seq')), parts along dimension 0, may hold values from -6 to 6
- latent_values: bfloat16 [65536, 2560], P(('cfg', 'seq')), parts along dimension 0, may hold values from -6 to 6
- prompt_keyvals: bfloat16 [2, 2048, 2560], P(None, ('cfg', 'seq')), parts along dimension 1, may hold values from -9 to 9
- block_lists: int32 [256, 8], P('seq'), may hold values from -1 to 255, as said below
- tile_segment: int32 [128], P('seq'), may hold values from 0 to 3
Outputs:
- attended: bfloat16 [65536, 2560], P(('cfg', 'seq')), parts along dimension 0
The draws below stay inside these ranges and needn't reach their ends.
There are 2 independent parts, one for each index of `cfg`. The reference program is written for one: setup_inputs(seed, part) draws one part's arguments, and reference() takes and returns one part's arrays. A program takes and returns all parts, laid end to end along the dimension named above; an argument that names none is the same for every part. Nothing has to cross between parts.
Inputs may be any that keep to these rules, and one draw needn't show every extreme that they name: `block_lists`: row b lists distinct key blocks, all held by indices of seq at most 3 away from the one holding query block b (each index holds 2 blocks in order); b itself comes first, used entries precede the -1 entries, and some row fills all 8.
All inputs are finite; a program needn't handle non-finite values.
Results may differ from the reference program's by a relative error of at most 0.0035.
Values may be sent and summed in bfloat16 or wider, within the bound.
No kernel may reach another device: no remote copies, remote signals or barrier semaphores. Data moves between devices by JAX's collectives and lax.ppermute only.
A program may use at most 128 MiB of HBM per device.

```python
import math
import jax
import jax.numpy as jnp
from jax import lax

HEADS = 20
HD = 128
TOK_DEV = 256
BLK = 128
REACH = 3
SLOTS = 8
SEGS = 4
TXT = 256
TOKENS = 32768
QBLOCKS = 256
TILES = 128
TXT_ALL = 1024


def shared_keys(key):
    base = jax.random.fold_in(key, 11)
    values = jnp.clip(jax.random.normal(base, (TOKENS, HEADS * HD), jnp.float32), -6.0, 6.0)
    return values


def draw_latent_keys(key, part):
    return shared_keys(key).astype(jnp.bfloat16)


def draw_queries(key, part):
    own = jnp.clip(jax.random.normal(jax.random.fold_in(key, 23), (TOKENS, HEADS * HD), jnp.float32), -6.0, 6.0)
    return own.astype(jnp.bfloat16)


def draw_tile_segment(key, part):
    key_base, key_pick = jax.random.split(jax.random.fold_in(key, 47), 2)
    segment_ids = jax.random.randint(key_base, (TILES,), 0, SEGS)
    chosen_tile = jax.random.randint(key_pick, (), 0, TILES)
    far_tile = (chosen_tile + TILES // 2) % TILES
    far_segment = far_tile * SEGS // TILES
    tiles_all = jnp.arange(TILES, dtype=jnp.int32)
    segment_ids = jnp.where(tiles_all == chosen_tile, far_segment, segment_ids)
    return segment_ids.astype(jnp.int32)


def draw_block_lists(key, part):
    per_device = TOK_DEV // BLK
    window = (2 * REACH + 1) * per_device
    rows = jnp.arange(QBLOCKS, dtype=jnp.int32)
    device = rows // per_device
    places = jnp.arange(window, dtype=jnp.int32)
    candidate = (device[:, None] - REACH) * per_device + places[None, :]
    valid = (candidate >= 0) & (candidate < QBLOCKS)
    distance = jnp.abs(places // per_device - REACH)
    key_noise, key_count, key_full, key_heavy = jax.random.split(jax.random.fold_in(key, 31), 4)
    noise = jax.random.randint(key_noise, (QBLOCKS, window), 0, 1000)
    score = noise - 250 * distance[None, :]
    score = jnp.where(candidate == rows[:, None], 100000, score)
    score = jnp.where(valid, score, -100000)
    score = score * window + places[None, :]
    unused, order = lax.top_k(score, SLOTS)
    chosen = jnp.take_along_axis(candidate, order, axis=1)
    chosen_valid = jnp.take_along_axis(valid, order, axis=1)
    heavy = jax.random.randint(key_heavy, (QBLOCKS // per_device,), 0, 4)
    light = jax.random.randint(key_count, (QBLOCKS,), SLOTS // 2, SLOTS)
    count = jnp.where(heavy[device] == 0, SLOTS, light)
    full_row = jax.random.randint(key_full, (), QBLOCKS // 2 - per_device, QBLOCKS // 2)
    count = jnp.where(rows == full_row, SLOTS, count)
    slot = jnp.arange(SLOTS, dtype=jnp.int32)
    keep = (slot[None, :] < count[:, None]) & chosen_valid
    return jnp.where(keep, chosen, -1).astype(jnp.int32)


def levels(own_key, dims, pieces, smallest, top_value):
    level, own = 1.0, jax.random.fold_in(own_key, 6)
    for dim, shards_of in pieces:
        steps = jnp.exp(jax.random.uniform(jax.random.fold_in(own, dim), (shards_of,), jnp.float32, smallest / len(pieces), top_value / len(pieces)))
        level = level * jnp.repeat(steps, dims[dim] // shards_of).reshape([-1 if axis == dim else 1 for axis in range(len(dims))])
    return level


def centred(rng, shape, deviation, reach, shards=(), held_as=jnp.bfloat16):
    array = deviation * jax.random.normal(rng, shape, jnp.float32)
    if shards:
        array = array * levels(rng, shape, shards, -0.22, 0.18)
    return jnp.clip(array, -reach, reach).astype(held_as)


def setup_inputs(seed: int = 0, part: int = 0) -> dict:
    key_of = jax.random.split(jax.random.key(seed), 7)
    part_keys = jax.random.split(jax.random.fold_in(key_of[6], part), 7)
    queries = draw_queries(jax.random.fold_in(jax.random.fold_in(key_of[6], part), 71), part)
    latent_keys = draw_latent_keys(jax.random.fold_in(jax.random.fold_in(key_of[6], part), 71), part)
    latent_values = centred(part_keys[2], (TOKENS, HEADS * HD), 1.0, 6.0, ((0, 128),))
    prompt_keyvals = centred(part_keys[3], (2, TXT_ALL, HEADS * HD), 1.5, 9.0, ((1, 128),))
    block_lists = draw_block_lists(jax.random.fold_in(key_of[6], 71), part)
    tile_segment = draw_tile_segment(jax.random.fold_in(key_of[6], 71), part)
    return {"queries": queries, "latent_keys": latent_keys, "latent_values": latent_values, "prompt_keyvals": prompt_keyvals, "block_lists": block_lists, "tile_segment": tile_segment}


def reference(queries, latent_keys, latent_values, prompt_keyvals, block_lists, tile_segment):
    per_device = TOK_DEV // BLK
    width = HEADS * HD
    scale = 1.0 / math.sqrt(HD)
    key_blocks = latent_keys.reshape(QBLOCKS, BLK, width)
    value_blocks = latent_values.reshape(QBLOCKS, BLK, width)
    query_blocks = queries.reshape(QBLOCKS, BLK, width)

    def one_block(index):
        lists = block_lists[index]
        valid = lists >= 0
        safe = jnp.where(valid, lists, 0).astype(jnp.int32)
        keys_sel = key_blocks[safe].reshape(SLOTS * BLK, width)
        values_sel = value_blocks[safe].reshape(SLOTS * BLK, width)
        segment = tile_segment[index // per_device]
        start = (segment * TXT).astype(jnp.int32)
        text_keys = lax.dynamic_slice_in_dim(prompt_keyvals[0], start, TXT, 0)
        text_values = lax.dynamic_slice_in_dim(prompt_keyvals[1], start, TXT, 0)
        all_keys = jnp.concatenate([keys_sel, text_keys], axis=0).astype(jnp.float32)
        all_values = jnp.concatenate([values_sel, text_values], axis=0).astype(jnp.float32)
        allowed = jnp.concatenate([jnp.repeat(valid, BLK), jnp.ones((TXT,), dtype=bool)])
        query_f = query_blocks[index].astype(jnp.float32).reshape(BLK, HEADS, HD)
        key_f = all_keys.reshape(-1, HEADS, HD)
        value_f = all_values.reshape(-1, HEADS, HD)
        scores = jnp.einsum('qhd,khd->hqk', query_f, key_f) * scale
        mask = allowed[None, None, :]
        top = lax.optimization_barrier(jnp.max(jnp.where(mask, scores, -jnp.inf), axis=2, keepdims=True))
        weights = jnp.where(mask, jnp.exp(scores - top), 0.0)
        total = lax.optimization_barrier(jnp.sum(weights, axis=2, keepdims=True))
        rounded = lax.optimization_barrier(weights.astype(jnp.bfloat16)).astype(jnp.float32)
        mixed = jnp.einsum('hqk,khd->hqd', rounded, value_f) / total
        return jnp.transpose(mixed, (1, 0, 2)).reshape(BLK, width).astype(jnp.bfloat16)
    result = lax.map(one_block, jnp.arange(QBLOCKS, dtype=jnp.int32))
    return result.reshape(TOKENS, width)
```

```python
import functools
import math

import jax
import jax.numpy as jnp
from jax import lax
from jax.experimental import pallas as pl
from jax.experimental.pallas import tpu as pltpu
from jax.sharding import PartitionSpec as P

HD = 128
BLK = 128
TOK = 256
ZN, YN, XN, CN = 8, 4, 2, 2
ROWS = ZN * YN
HALF = 10
CHUNKS = (3, 4, 3)
NEG = -1e30
C2 = math.log2(math.e) / math.sqrt(HD)


def place(row, x, core):
    return ((row % ROWS) * XN + x % XN) * CN + core % CN


DEVICES = [(r, x, c) for r in range(ROWS) for x in range(XN) for c in range(CN)]


def route(to):
    return [(place(*d), place(*to(*d))) for d in DEVICES]


ACROSS = route(lambda r, x, c: (r, 1 - x, c))
CORES = route(lambda r, x, c: (r, x, 1 - c))
OUTWARD = route(lambda r, x, c: (r + (1 if c else -1), x, c))
INWARD = route(lambda r, x, c: (r + (-1 if c else 1), x, c))
ZUP = route(lambda r, x, c: (r + YN, x, c))
ZDOWN = route(lambda r, x, c: (r - YN, x, c))
PLANES = [
    [place(z * YN + y, x, c) for y in range(YN) for x in range(XN)]
    for z in range(ZN)
    for c in range(CN)
]


def send(block, to):
    return lax.ppermute(block, "seq", to)


def attend_kernel(
    half_ref, slots_ref, valid_ref, text_at_ref,
    q_own, q_far, k_own, v_own, far, out_own, out_far, mid, cc_fix, cc_part, text, cc_text,
    o_own, o_far, keys, values,
):
    tiles = [
        (k_own, v_own),
        (far.at[0], far.at[1]),
        (out_own.at[0], out_own.at[1]),
        (out_far.at[0], out_far.at[1]),
        (mid.at[0], mid.at[1]),
        (cc_fix.at[0, 0], cc_fix.at[0, 1]),
        (cc_part.at[0, 0], cc_part.at[0, 1]),
        (cc_fix.at[1, 0], cc_fix.at[1, 1]),
        (cc_part.at[1, 0], cc_part.at[1, 1]),
        (cc_part.at[2, 0], cc_part.at[2, 1]),
    ]
    for at, (k, v) in enumerate(tiles):
        keys[at * TOK : (at + 1) * TOK, :] = k[...]
        values[at * TOK : (at + 1) * TOK, :] = v[...]
    for tile, (q_ref, o_ref) in enumerate(((q_own, o_own), (q_far, o_far))):
        first, second = text_at_ref[tile, 0], text_at_ref[tile, 1]
        text_k = [ref[at, 0] for ref in (text, cc_text) for at in (first, second)]
        text_v = [ref[at, 1] for ref in (text, cc_text) for at in (first, second)]
        for block in range(TOK // BLK):
            row = tile * 2 + block
            rows = slice(block * BLK, (block + 1) * BLK)
            starts = [pl.multiple_of(slots_ref[row, s] * BLK, BLK) for s in range(8)]
            all_k = jnp.concatenate([keys[pl.ds(at, BLK), :] for at in starts] + text_k, axis=0)
            all_v = jnp.concatenate([values[pl.ds(at, BLK), :] for at in starts] + text_v, axis=0)
            scores = lax.dot_general(
                q_ref[rows, :], all_k, (((1,), (1,)), ((), ())), preferred_element_type=jnp.float32
            )
            scores = jnp.concatenate(
                [scores[:, :BLK]]
                + [
                    jnp.where(valid_ref[row, s] > 0, scores[:, s * BLK : (s + 1) * BLK], NEG)
                    for s in range(1, 8)
                ]
                + [scores[:, 8 * BLK :]],
                axis=1,
            )
            top = jnp.max(scores, axis=1, keepdims=True)
            weights = jnp.exp2((scores - top) * C2)
            total = jnp.sum(weights, axis=1, keepdims=True)
            mixed = jnp.dot(weights.astype(jnp.bfloat16), all_v, preferred_element_type=jnp.float32)
            o_ref[rows, :] = (mixed / total).astype(jnp.bfloat16)


def attend(first, heads, scalars, q_own, q_far, k_own, v_own, far, out_own, out_far, mid, cc_fix, cc_part, text, cc_text):
    def whole(i, half, *_):
        return (0, half[0] * HALF + first + i)

    def halved(lead):
        return lambda i, *_: (0,) * lead + (first + i,)

    def chunk(lead):
        return lambda i, *_: (0,) * lead + (i,)

    specs = [
        pl.BlockSpec((TOK, HD), whole),
        pl.BlockSpec((TOK, HD), halved(1)),
        pl.BlockSpec((TOK, HD), whole),
        pl.BlockSpec((TOK, HD), whole),
        pl.BlockSpec((2, TOK, HD), chunk(2)),
        pl.BlockSpec((2, TOK, HD), halved(2)),
        pl.BlockSpec((2, TOK, HD), chunk(2)),
        pl.BlockSpec((2, TOK, HD), chunk(2)),
        pl.BlockSpec((2, 2, TOK, HD), halved(3)),
        pl.BlockSpec((3, 2, TOK, HD), chunk(3)),
        pl.BlockSpec((ZN, 2, 64, HD), halved(3)),
        pl.BlockSpec((ZN, 2, 64, HD), halved(3)),
    ]
    out = jax.ShapeDtypeStruct((TOK, heads * HD), jnp.bfloat16)
    return pl.pallas_call(
        attend_kernel,
        out_shape=(out, out),
        grid_spec=pltpu.PrefetchScalarGridSpec(
            num_scalar_prefetch=4,
            grid=(heads,),
            in_specs=specs,
            out_specs=(pl.BlockSpec((TOK, HD), chunk(1)), pl.BlockSpec((TOK, HD), chunk(1))),
            scratch_shapes=[
                pltpu.VMEM((10 * TOK, HD), jnp.bfloat16),
                pltpu.VMEM((10 * TOK, HD), jnp.bfloat16),
            ],
        ),
        compiler_params=pltpu.CompilerParams(vmem_limit_bytes=32 * 1024 * 1024),
        cost_estimate=pl.CostEstimate(
            flops=heads * 4 * 128 * 1280 * 128 * 4,
            bytes_accessed=heads * 2200000,
            transcendentals=heads * 4 * 128 * 1280,
        ),
        name="attend",
    )(*scalars, q_own, q_far, k_own, v_own, far, out_own, out_far, mid, cc_fix, cc_part, text, cc_text)


def on_device(queries, latent_keys, latent_values, prompt_keyvals, block_lists, tile_segment):
    width = HALF * HD
    device = lax.axis_index("seq")
    core, x, row = device % CN, device // CN % XN, device // (CN * XN)
    z = row // YN

    def half_of(array, which):
        return lax.dynamic_slice_in_dim(array, which * width, width, array.ndim - 1)

    own_table = jnp.concatenate(
        [block_lists, jnp.broadcast_to(tile_segment[:, None], (2, 8))], axis=1
    )
    table = jnp.concatenate([own_table, send(own_table, ACROSS)], axis=0)
    lists, segments = table[:, :8], table[::2, 8]

    def held(which):
        side = 2 * which - 1
        return [
            2 * x + which,
            2 * (1 - x) + which,
            2 * x + which - 4 * side,
            2 * (1 - x) + which - 4 * side,
            2 - which + 4 * side,
        ]

    offsets = jnp.stack(held(core) + held(1 - core))
    wanted = lists // 2 - 4 * row
    position = jnp.argmax(wanted[:, :, None] == offsets[None, None, :], axis=2).astype(jnp.int32)
    valid = (lists >= 0).astype(jnp.int32)
    slots = jnp.where(lists >= 0, position * 2 + lists % 2, 0)
    text_at = (2 * segments[:, None] + jnp.arange(2)[None, :] - z) % ZN
    scalars = (x[None].astype(jnp.int32), slots, valid, text_at.astype(jnp.int32))

    halves = jnp.stack([prompt_keyvals[..., :width], prompt_keyvals[..., width:]])
    plane = lax.all_to_all(
        jnp.concatenate([halves] * YN, axis=0), "seq", 0, 0, axis_index_groups=PLANES
    )
    plane = jnp.swapaxes(plane, 0, 1).reshape(2, 64, width)
    ups, downs = [plane], [plane]
    for _ in range(4):
        ups.append(send(ups[-1], ZUP))
    for _ in range(3):
        downs.append(send(downs[-1], ZDOWN))
    text = jnp.stack([plane, downs[1], downs[2], downs[3], ups[4], ups[3], ups[2], ups[1]])
    cc_text = send(text, CORES)

    kv_own = jnp.stack([half_of(latent_keys, x), half_of(latent_values, x)])
    kv_give = jnp.stack([half_of(latent_keys, 1 - x), half_of(latent_values, 1 - x)])
    out_own = send(kv_own, OUTWARD)
    cc_fix = send(jnp.stack([kv_own, out_own]), CORES)
    q_far = send(half_of(queries, 1 - x), ACROSS)
    results = []
    first = 0
    for heads in CHUNKS:
        cols = slice(first * HD, (first + heads) * HD)
        far = send(kv_give[..., cols], ACROSS)
        out_far = send(far, OUTWARD)
        mid = send(jnp.where(x != core, kv_own[..., cols], far), INWARD)
        cc_part = send(jnp.stack([far, out_far, mid]), CORES)
        mine, theirs = attend(
            first, heads, scalars, queries, q_far, latent_keys, latent_values,
            far, out_own, out_far, mid, cc_fix, cc_part, text, cc_text,
        )
        results.append((mine, send(theirs, ACROSS)))
        first += heads
    mine = jnp.concatenate([m for m, _ in results], axis=1)
    back = jnp.concatenate([b for _, b in results], axis=1)
    left, right = jnp.where(x == 0, mine, back), jnp.where(x == 0, back, mine)
    return jnp.concatenate([left, right], axis=1)


def solution(mesh):
    in_specs = (
        P(("cfg", "seq"), None),
        P(("cfg", "seq"), None),
        P(("cfg", "seq"), None),
        P(None, ("cfg", "seq"), None),
        P("seq", None),
        P("seq"),
    )
    out_specs = P(("cfg", "seq"), None)
    return jax.shard_map(
        on_device, mesh=mesh, in_specs=in_specs, out_specs=out_specs, check_vma=False
    )
```

```python
import functools
import math

import jax
import jax.numpy as jnp
from jax import lax
from jax.experimental import pallas as pl
from jax.experimental.pallas import tpu as pltpu
from jax.sharding import PartitionSpec as P

HD = 128
BLK = 128
TOK = 256
ZN, YN, XN, CN = 8, 4, 2, 2
ROWS = ZN * YN
HALF = 10
CHUNKS = (6, 4)
NEG = -1e30
C2 = math.log2(math.e) / math.sqrt(HD)


def place(row, x, core):
    return ((row % ROWS) * XN + x % XN) * CN + core % CN


DEVICES = [(r, x, c) for r in range(ROWS) for x in range(XN) for c in range(CN)]


def route(to):
    return [(place(*d), place(*to(*d))) for d in DEVICES]


ACROSS = route(lambda r, x, c: (r, 1 - x, c))
CORES = route(lambda r, x, c: (r, x, 1 - c))
OUTWARD = route(lambda r, x, c: (r + (1 if c else -1), x, c))
INWARD = route(lambda r, x, c: (r + (-1 if c else 1), x, c))
ZUP = route(lambda r, x, c: (r + YN, x, c))
ZDOWN = route(lambda r, x, c: (r - YN, x, c))


def pack_kernel(*refs):
    whole = refs[-1]
    for i, block in enumerate(refs[:-1]):

        @pl.when(pl.program_id(0) == i)
        def _():
            whole[...] = block[...]


def pack(*blocks):
    shape = blocks[0].shape
    zeros = (0,) * len(shape)
    return pl.pallas_call(
        pack_kernel,
        out_shape=jax.ShapeDtypeStruct((len(blocks), *shape), blocks[0].dtype),
        grid=(len(blocks),),
        in_specs=[pl.BlockSpec(shape, lambda i: zeros)] * len(blocks),
        out_specs=pl.BlockSpec((None, *shape), lambda i: (i, *zeros)),
        compiler_params=pltpu.CompilerParams(vmem_limit_bytes=32 * 1024 * 1024),
        name="pack",
    )(*blocks)


def gather_kernel(*refs):
    whole = refs[-1]
    for i, pair in enumerate(refs[:-1]):
        whole[i] = pair[...]


def gather_heads(first, heads, *pairs):
    pair = (2, TOK, HD)

    def spec(width):
        start = first if width == HALF * HD else 0
        return pl.BlockSpec(pair, lambda i: (0, 0, start + i))

    return pl.pallas_call(
        gather_kernel,
        out_shape=jax.ShapeDtypeStruct((len(pairs), 2, TOK, heads * HD), jnp.bfloat16),
        grid=(heads,),
        in_specs=[spec(p.shape[-1]) for p in pairs],
        out_specs=pl.BlockSpec((len(pairs), *pair), lambda i: (0, 0, 0, i)),
        compiler_params=pltpu.CompilerParams(vmem_limit_bytes=32 * 1024 * 1024),
        name="gather_heads",
    )(*pairs)


def softened(parts, top):
    weights = [jnp.exp2((part - top) * C2) for part in parts]
    total = jnp.sum(functools.reduce(jnp.add, weights), axis=1, keepdims=True)
    return jnp.concatenate([w.astype(jnp.bfloat16) for w in weights], axis=1), total


def scored(query, keys):
    return lax.dot_general(query, keys, (((1,), (1,)), ((), ())), preferred_element_type=jnp.float32)


UNITS = [
    (tile, slice(block * BLK, (block + 1) * BLK), tile * 2 + block)
    for tile in range(2)
    for block in range(TOK // BLK)
]


def latent_kernel(
    half_ref, slots_ref, valid_ref, text_at_ref,
    q_own, q_far, k_own, v_own, far, out_own, out_far, mid, cc_part,
    sums, stats, keys, values,
):
    tiles = [
        (k_own, v_own),
        *[(pair.at[0], pair.at[1]) for pair in (far, out_own, out_far, mid)],
        *[(cc_part.at[i, 0], cc_part.at[i, 1]) for i in range(5)],
    ]
    for at, (k, v) in enumerate(tiles):
        keys[at * TOK : (at + 1) * TOK, :] = k[...]
        values[at * TOK : (at + 1) * TOK, :] = v[...]

    def listed(row, store):
        starts = [pl.multiple_of(slots_ref[row, s] * BLK, BLK) for s in range(8)]
        return jnp.concatenate([store[pl.ds(at, BLK), :] for at in starts], axis=0)

    def score(unit):
        tile, rows, row = unit
        scores = scored((q_own, q_far)[tile][rows, :], listed(row, keys))
        parts = [scores[:, s * BLK : (s + 1) * BLK] for s in range(8)]
        for s in range(1, 8):
            parts[s] = jnp.where(valid_ref[row, s] > 0, parts[s], NEG)
        return parts

    left = lax.broadcasted_iota(jnp.int32, (BLK, HD), 1) < HD // 2
    ahead = score(UNITS[0])
    for unit, later in zip(UNITS, UNITS[1:] + [None]):
        parts, ahead = ahead, score(later) if later else None
        tile, rows, row = unit
        top = jnp.max(functools.reduce(jnp.maximum, parts), axis=1, keepdims=True)
        rounded, total = softened(parts, top)
        sums[tile, rows, :] = jnp.dot(
            rounded, listed(row, values), preferred_element_type=jnp.float32
        )
        stats[tile, rows, :] = jnp.where(left, top, total)


def text_kernel(
    half_ref, slots_ref, valid_ref, text_at_ref,
    q_own, q_far, sums, stats, near, last, cc_near, cc_last, o_own, o_far, keys, values,
):
    for core, (most, other) in enumerate(((near, last), (cc_near, cc_last))):
        for at, plane in enumerate([most.at[i] for i in range(7)] + [other]):
            to = at * BLK + core * 64
            keys[to : to + 64, :] = plane[0]
            values[to : to + 64, :] = plane[1]

    def listed(tile, store):
        starts = [pl.multiple_of(text_at_ref[tile, i] * BLK, BLK) for i in range(2)]
        return jnp.concatenate([store[pl.ds(at, BLK), :] for at in starts], axis=0)

    scores = [
        scored((q_own, q_far)[tile][rows, :], listed(tile, keys)) for tile, rows, row in UNITS
    ]
    parts = [[score[:, :BLK], score[:, BLK:]] for score in scores]
    before = [stats[tile, rows, :1] for tile, rows, row in UNITS]
    ends = slice(HD // 2, HD // 2 + 1)
    totals_before = [stats[tile, rows, ends] for tile, rows, row in UNITS]
    tops = [
        jnp.maximum(old, jnp.max(jnp.maximum(*part), axis=1, keepdims=True))
        for old, part in zip(before, parts)
    ]
    softs = [softened(part, top) for part, top in zip(parts, tops)]
    fades = [jnp.exp2((old - top) * C2) for old, top in zip(before, tops)]
    mixes = [
        jnp.dot(rounded, listed(tile, values), preferred_element_type=jnp.float32)
        for (rounded, _), (tile, rows, row) in zip(softs, UNITS)
    ]
    for i, (tile, rows, row) in enumerate(UNITS):
        total = totals_before[i] * fades[i] + softs[i][1]
        mixed = (sums[tile, rows, :] * fades[i] + mixes[i]) / total
        (o_own, o_far)[tile][rows, :] = mixed.astype(jnp.bfloat16)


def specs_of(first):
    def whole(i, half, *_):
        return (0, half[0] * HALF + first + i)

    def halved(lead):
        return lambda i, *_: (0,) * lead + (first + i,)

    def chunk(lead):
        return lambda i, *_: (0,) * lead + (i,)

    return whole, halved, chunk


def call(kernel, name, heads, keys, in_specs, out_shape, out_specs, rows, arguments):
    return pl.pallas_call(
        kernel,
        out_shape=out_shape,
        grid_spec=pltpu.PrefetchScalarGridSpec(
            num_scalar_prefetch=4,
            grid=(heads,),
            in_specs=in_specs,
            out_specs=out_specs,
            scratch_shapes=[pltpu.VMEM((rows, HD), jnp.bfloat16)] * 2,
        ),
        compiler_params=pltpu.CompilerParams(vmem_limit_bytes=56 * 1024 * 1024),
        cost_estimate=pl.CostEstimate(
            flops=heads * 4 * BLK * keys * HD * 4 * 6,
            bytes_accessed=heads * keys * 2000,
            transcendentals=heads * 4 * BLK * keys,
        ),
        name=name,
    )(*arguments)


def latent(first, heads, scalars, *arrays):
    whole, halved, chunk = specs_of(first)
    pair = (2, TOK, HD)
    in_specs = [
        pl.BlockSpec((TOK, HD), whole),
        pl.BlockSpec((TOK, HD), halved(1)),
        pl.BlockSpec((TOK, HD), whole),
        pl.BlockSpec((TOK, HD), whole),
        pl.BlockSpec(pair, chunk(2)),
        pl.BlockSpec(pair, halved(2)),
        pl.BlockSpec(pair, chunk(2)),
        pl.BlockSpec(pair, chunk(2)),
        pl.BlockSpec((5, *pair), chunk(3)),
    ]
    out = jax.ShapeDtypeStruct((2, TOK, heads * HD), jnp.float32)
    out_specs = (pl.BlockSpec(pair, chunk(2)), pl.BlockSpec(pair, chunk(2)))
    return call(
        latent_kernel, "latent", heads, 1024, in_specs, (out, out), out_specs, 10 * TOK,
        (*scalars, *arrays),
    )


def finish(first, heads, scalars, *arrays):
    whole, halved, chunk = specs_of(first)
    in_specs = [
        pl.BlockSpec((TOK, HD), whole),
        pl.BlockSpec((TOK, HD), halved(1)),
        pl.BlockSpec((2, TOK, HD), chunk(2)),
        pl.BlockSpec((2, TOK, HD), chunk(2)),
        *[pl.BlockSpec((7, 2, 64, HD), halved(3)), pl.BlockSpec((2, 64, HD), halved(2))] * 2,
    ]
    out = jax.ShapeDtypeStruct((TOK, heads * HD), jnp.bfloat16)
    out_specs = (pl.BlockSpec((TOK, HD), chunk(1)), pl.BlockSpec((TOK, HD), chunk(1)))
    return call(
        text_kernel, "finish", heads, 256, in_specs, (out, out), out_specs, ZN * BLK,
        (*scalars, *arrays),
    )


PLANES = [
    [place(z * YN + y, x, c) for y in range(YN) for x in range(XN)]
    for z in range(ZN)
    for c in range(CN)
]


def send(what, block, to):
    with jax.named_scope(what):
        return lax.ppermute(block, "seq", to)


def on_device(queries, latent_keys, latent_values, prompt_keyvals, block_lists, tile_segment):
    width = HALF * HD
    device = lax.axis_index("seq")
    core, x, row = device % CN, device // CN % XN, device // (CN * XN)
    z = row // YN

    def half_of(array, which, first=0, heads=HALF):
        start = which * width + first * HD
        return lax.dynamic_slice_in_dim(array, start, heads * HD, array.ndim - 1)

    def pair_of(which, first=0, heads=HALF):
        return jnp.stack([half_of(a, which, first, heads) for a in (latent_keys, latent_values)])

    def whereabouts(*tables):
        table = jnp.concatenate(tables, axis=0)
        lists, segments = table[:, :8], table[::2, 8]

        def held(which):
            side = 2 * which - 1
            return [
                2 * x + which,
                2 * (1 - x) + which,
                2 * x + which - 4 * side,
                2 * (1 - x) + which - 4 * side,
                2 - which + 4 * side,
            ]

        offsets = jnp.stack(held(core) + held(1 - core))
        wanted = lists // 2 - 4 * row
        position = jnp.argmax(wanted[:, :, None] == offsets[None, None, :], axis=2).astype(jnp.int32)
        valid = (lists >= 0).astype(jnp.int32)
        slots = jnp.where(lists >= 0, position * 2 + lists % 2, 0)
        ahead = (2 * segments[:, None] + jnp.arange(2)[None, :] - z) % ZN
        order = (0, 1, 2, 3, 7, 6, 5, 4)
        text_at = sum(jnp.where(ahead == k, at, 0) for k, at in enumerate(order))
        return (x[None].astype(jnp.int32), slots, valid, text_at.astype(jnp.int32))

    firsts = [sum(CHUNKS[:i]) for i in range(len(CHUNKS))]
    gives = [pair_of(1 - x, f, h) for f, h in zip(firsts, CHUNKS)]
    kv_own = pair_of(x)

    own_table = jnp.concatenate(
        [block_lists, jnp.broadcast_to(tile_segment[:, None], (2, 8))], axis=1
    )
    far_table = send("table", own_table, ACROSS)
    halves = jnp.stack([prompt_keyvals[..., :width], prompt_keyvals[..., width:]])
    spread = jnp.broadcast_to(halves[None], (YN, *halves.shape))
    plane = lax.all_to_all(
        spread.reshape(YN * XN, *halves.shape[1:]), "seq", 0, 0, axis_index_groups=PLANES
    )
    plane = jnp.swapaxes(plane, 0, 1).reshape(2, 64, width)
    far1 = send("far", gives[0], ACROSS)
    kv_own, plane, far_table = lax.optimization_barrier((kv_own, plane, far_table))
    scalars = whereabouts(own_table, far_table)
    out_own = send("out_own", kv_own, OUTWARD)
    q_far = send("q_far", half_of(queries, 1 - x), ACROSS)
    up1, down1 = send("text_up", plane, ZUP), send("text_down", plane, ZDOWN)
    give2, up1, down1, far1, out_own, kv_own, q_far, *scalars = lax.optimization_barrier(
        (gives[1], up1, down1, far1, out_own, kv_own, q_far, *scalars)
    )

    def between(first, heads, far):
        return jnp.where(x != core, kv_own[..., first * HD : (first + heads) * HD], far)

    def swapped(i, far, out_far, mid):
        held_here = gather_heads(firsts[i], CHUNKS[i], kv_own, far, out_own, out_far, mid)
        return send("cc_part", held_here, CORES)

    def attended(i, far, out_far, mid, cc_part):
        return latent(
            firsts[i], CHUNKS[i], scalars, queries, q_far, latent_keys, latent_values,
            far, out_own, out_far, mid, cc_part,
        )

    far2 = send("far", give2, ACROSS)
    out_far1 = send("out_far", far1, OUTWARD)
    mid1 = send("mid", between(firsts[0], CHUNKS[0], far1), INWARD)
    up2, down2 = send("text_up", up1, ZUP), send("text_down", down1, ZDOWN)
    far2, out_far1, mid1, up2, down2 = lax.optimization_barrier((far2, out_far1, mid1, up2, down2))

    out_far2 = send("out_far", far2, OUTWARD)
    mid2 = send("mid", between(firsts[1], CHUNKS[1], far2), INWARD)
    up3, down3 = send("text_up", up2, ZUP), send("text_down", down2, ZDOWN)
    sums1 = attended(0, far1, out_far1, mid1, swapped(0, far1, out_far1, mid1))
    out_far2, mid2, up3, down3, *sums1 = lax.optimization_barrier(
        (out_far2, mid2, up3, down3, *sums1)
    )

    up4 = send("text_up", up3, ZUP)
    near = pack(plane, down1, down2, down3, up1, up2, up3)
    cc_near = send("cc_text", near, CORES)
    sums2 = attended(1, far2, out_far2, mid2, swapped(1, far2, out_far2, mid2))
    up4, _, _ = lax.optimization_barrier((up4, *sums2))
    cc_last = send("cc_text", up4, CORES)
    text = (near, up4, cc_near, cc_last)
    results = []
    for first, heads, sums in zip(firsts, CHUNKS, (sums1, sums2)):
        mine, theirs = finish(first, heads, scalars, queries, q_far, *sums, *text)
        results.append((mine, send("back", theirs, ACROSS)))
    mine = jnp.concatenate([m for m, _ in results], axis=1)
    back = jnp.concatenate([b for _, b in results], axis=1)
    left, right = jnp.where(x == 0, mine, back), jnp.where(x == 0, back, mine)
    return jnp.concatenate([left, right], axis=1)


def solution(mesh):
    in_specs = (
        P(("cfg", "seq"), None),
        P(("cfg", "seq"), None),
        P(("cfg", "seq"), None),
        P(None, ("cfg", "seq"), None),
        P("seq", None),
        P("seq"),
    )
    out_specs = P(("cfg", "seq"), None)
    return jax.shard_map(
        on_device, mesh=mesh, in_specs=in_specs, out_specs=out_specs, check_vma=False
    )
```

```python
import functools
import math

import jax
import jax.numpy as jnp
from jax import lax
from jax.experimental import pallas as pl
from jax.experimental.pallas import tpu as pltpu
from jax.sharding import PartitionSpec as P

HD = 128
BLK = 128
TOK = 256
ZN, YN, XN, CN = 8, 4, 2, 2
ROWS = ZN * YN
HALF = 10
CHUNKS = (6, 4)
NEG = -1e30
C2 = math.log2(math.e) / math.sqrt(HD)


def place(row, x, core):
    return ((row % ROWS) * XN + x % XN) * CN + core % CN


DEVICES = [(r, x, c) for r in range(ROWS) for x in range(XN) for c in range(CN)]


def route(to):
    return [(place(*d), place(*to(*d))) for d in DEVICES]


ACROSS = route(lambda r, x, c: (r, 1 - x, c))
CORES = route(lambda r, x, c: (r, x, 1 - c))
OUTWARD = route(lambda r, x, c: (r + (1 if c else -1), x, c))
INWARD = route(lambda r, x, c: (r + (-1 if c else 1), x, c))
MAJOR = route(lambda r, x, c: (r + (YN if r % YN < 2 else -YN), x, c))
MINOR = route(lambda r, x, c: (r - (YN if r % YN < 2 else -YN), x, c))


def pack_kernel(*refs):
    whole = refs[-1]
    for i, block in enumerate(refs[:-1]):

        @pl.when(pl.program_id(0) == i)
        def _():
            whole[...] = block[...]


def pack(*blocks):
    shape = blocks[0].shape
    zeros = (0,) * len(shape)
    return pl.pallas_call(
        pack_kernel,
        out_shape=jax.ShapeDtypeStruct((len(blocks), *shape), blocks[0].dtype),
        grid=(len(blocks),),
        in_specs=[pl.BlockSpec(shape, lambda i: zeros)] * len(blocks),
        out_specs=pl.BlockSpec((None, *shape), lambda i: (i, *zeros)),
        compiler_params=pltpu.CompilerParams(vmem_limit_bytes=32 * 1024 * 1024),
        name="pack",
    )(*blocks)


def gather_kernel(*refs):
    whole = refs[-1]
    for i, pair in enumerate(refs[:-1]):
        whole[i] = pair[...]


def gather_heads(first, heads, *pairs):
    pair = (2, TOK, HD)

    def spec(width):
        start = first if width == HALF * HD else 0
        return pl.BlockSpec(pair, lambda i: (0, 0, start + i))

    return pl.pallas_call(
        gather_kernel,
        out_shape=jax.ShapeDtypeStruct((len(pairs), 2, TOK, heads * HD), jnp.bfloat16),
        grid=(heads,),
        in_specs=[spec(p.shape[-1]) for p in pairs],
        out_specs=pl.BlockSpec((len(pairs), *pair), lambda i: (0, 0, 0, i)),
        compiler_params=pltpu.CompilerParams(vmem_limit_bytes=32 * 1024 * 1024),
        name="gather_heads",
    )(*pairs)


def softened(parts, top):
    weights = [jnp.exp2((part - top) * C2) for part in parts]
    total = jnp.sum(functools.reduce(jnp.add, weights), axis=1, keepdims=True)
    return jnp.concatenate([w.astype(jnp.bfloat16) for w in weights], axis=1), total


def scored(query, keys):
    return lax.dot_general(query, keys, (((1,), (1,)), ((), ())), preferred_element_type=jnp.float32)


UNITS = [
    (tile, slice(block * BLK, (block + 1) * BLK), tile * 2 + block)
    for tile in range(2)
    for block in range(TOK // BLK)
]


def latent_kernel(
    half_ref, slots_ref, valid_ref, text_at_ref,
    q_own, q_far, k_own, v_own, far, out_own, out_far, mid, cc_part,
    sums, stats, keys, values,
):
    tiles = [
        (k_own, v_own),
        *[(pair.at[0], pair.at[1]) for pair in (far, out_own, out_far, mid)],
        *[(cc_part.at[i, 0], cc_part.at[i, 1]) for i in range(5)],
    ]
    for at, (k, v) in enumerate(tiles):
        keys[at * TOK : (at + 1) * TOK, :] = k[...]
        values[at * TOK : (at + 1) * TOK, :] = v[...]

    def listed(row, store):
        starts = [pl.multiple_of(slots_ref[row, s] * BLK, BLK) for s in range(8)]
        return jnp.concatenate([store[pl.ds(at, BLK), :] for at in starts], axis=0)

    def score(unit):
        tile, rows, row = unit
        scores = scored((q_own, q_far)[tile][rows, :], listed(row, keys))
        parts = [scores[:, s * BLK : (s + 1) * BLK] for s in range(8)]
        for s in range(1, 8):
            parts[s] = jnp.where(valid_ref[row, s] > 0, parts[s], NEG)
        return parts

    left = lax.broadcasted_iota(jnp.int32, (BLK, HD), 1) < HD // 2
    ahead = score(UNITS[0])
    for unit, later in zip(UNITS, UNITS[1:] + [None]):
        parts, ahead = ahead, score(later) if later else None
        tile, rows, row = unit
        top = jnp.max(functools.reduce(jnp.maximum, parts), axis=1, keepdims=True)
        rounded, total = softened(parts, top)
        sums[tile, rows, :] = jnp.dot(
            rounded, listed(row, values), preferred_element_type=jnp.float32
        )
        stats[tile, rows, :] = jnp.where(left, top, total)


def text_kernel(
    half_ref, slots_ref, valid_ref, text_at_ref,
    q_own, q_far, sums, stats, near, last, cc_near, cc_last, o_own, o_far, keys, values,
):
    for core, (most, other) in enumerate(((near, last), (cc_near, cc_last))):
        planes = [most.at[i] for i in range(6)] + [other.at[i] for i in range(2)]
        for at, plane in enumerate(planes):
            to = at * BLK + core * 64
            keys[to : to + 64, :] = plane[0]
            values[to : to + 64, :] = plane[1]

    def listed(tile, store):
        starts = [pl.multiple_of(text_at_ref[tile, i] * BLK, BLK) for i in range(2)]
        return jnp.concatenate([store[pl.ds(at, BLK), :] for at in starts], axis=0)

    scores = [
        scored((q_own, q_far)[tile][rows, :], listed(tile, keys)) for tile, rows, row in UNITS
    ]
    parts = [[score[:, :BLK], score[:, BLK:]] for score in scores]
    before = [stats[tile, rows, :1] for tile, rows, row in UNITS]
    ends = slice(HD // 2, HD // 2 + 1)
    totals_before = [stats[tile, rows, ends] for tile, rows, row in UNITS]
    tops = [
        jnp.maximum(old, jnp.max(jnp.maximum(*part), axis=1, keepdims=True))
        for old, part in zip(before, parts)
    ]
    softs = [softened(part, top) for part, top in zip(parts, tops)]
    fades = [jnp.exp2((old - top) * C2) for old, top in zip(before, tops)]
    mixes = [
        jnp.dot(rounded, listed(tile, values), preferred_element_type=jnp.float32)
        for (rounded, _), (tile, rows, row) in zip(softs, UNITS)
    ]
    for i, (tile, rows, row) in enumerate(UNITS):
        total = totals_before[i] * fades[i] + softs[i][1]
        mixed = (sums[tile, rows, :] * fades[i] + mixes[i]) / total
        (o_own, o_far)[tile][rows, :] = mixed.astype(jnp.bfloat16)


def specs_of(first):
    def whole(i, half, *_):
        return (0, half[0] * HALF + first + i)

    def halved(lead):
        return lambda i, *_: (0,) * lead + (first + i,)

    def chunk(lead):
        return lambda i, *_: (0,) * lead + (i,)

    return whole, halved, chunk


def call(kernel, name, heads, keys, in_specs, out_shape, out_specs, rows, arguments):
    return pl.pallas_call(
        kernel,
        out_shape=out_shape,
        grid_spec=pltpu.PrefetchScalarGridSpec(
            num_scalar_prefetch=4,
            grid=(heads,),
            in_specs=in_specs,
            out_specs=out_specs,
            scratch_shapes=[pltpu.VMEM((rows, HD), jnp.bfloat16)] * 2,
        ),
        compiler_params=pltpu.CompilerParams(vmem_limit_bytes=56 * 1024 * 1024),
        cost_estimate=pl.CostEstimate(
            flops=heads * 4 * BLK * keys * HD * 4 * 6,
            bytes_accessed=heads * keys * 2000,
            transcendentals=heads * 4 * BLK * keys,
        ),
        name=name,
    )(*arguments)


def latent(first, heads, scalars, *arrays):
    whole, halved, chunk = specs_of(first)
    pair = (2, TOK, HD)
    in_specs = [
        pl.BlockSpec((TOK, HD), whole),
        pl.BlockSpec((TOK, HD), halved(1)),
        pl.BlockSpec((TOK, HD), whole),
        pl.BlockSpec((TOK, HD), whole),
        pl.BlockSpec(pair, chunk(2)),
        pl.BlockSpec(pair, halved(2)),
        pl.BlockSpec(pair, chunk(2)),
        pl.BlockSpec(pair, chunk(2)),
        pl.BlockSpec((5, *pair), chunk(3)),
    ]
    out = jax.ShapeDtypeStruct((2, TOK, heads * HD), jnp.float32)
    out_specs = (pl.BlockSpec(pair, chunk(2)), pl.BlockSpec(pair, chunk(2)))
    return call(
        latent_kernel, "latent", heads, 1024, in_specs, (out, out), out_specs, 10 * TOK,
        (*scalars, *arrays),
    )


def finish(first, heads, scalars, *arrays):
    whole, halved, chunk = specs_of(first)
    in_specs = [
        pl.BlockSpec((TOK, HD), whole),
        pl.BlockSpec((TOK, HD), halved(1)),
        pl.BlockSpec((2, TOK, HD), chunk(2)),
        pl.BlockSpec((2, TOK, HD), chunk(2)),
        *[pl.BlockSpec((n, 2, 64, HD), halved(3)) for n in (6, 2, 6, 2)],
    ]
    out = jax.ShapeDtypeStruct((TOK, heads * HD), jnp.bfloat16)
    out_specs = (pl.BlockSpec((TOK, HD), chunk(1)), pl.BlockSpec((TOK, HD), chunk(1)))
    return call(
        text_kernel, "finish", heads, 256, in_specs, (out, out), out_specs, ZN * BLK,
        (*scalars, *arrays),
    )


PLANES = [
    [place(z * YN + y, x, c) for y in range(YN) for x in range(XN)]
    for z in range(ZN)
    for c in range(CN)
]


def send(what, block, to):
    with jax.named_scope(what):
        return lax.ppermute(block, "seq", to)


def on_device(queries, latent_keys, latent_values, prompt_keyvals, block_lists, tile_segment):
    width = HALF * HD
    device = lax.axis_index("seq")
    core, x, row = device % CN, device // CN % XN, device // (CN * XN)
    z = row // YN

    def half_of(array, which, first=0, heads=HALF):
        start = which * width + first * HD
        return lax.dynamic_slice_in_dim(array, start, heads * HD, array.ndim - 1)

    def pair_of(which, first=0, heads=HALF):
        return jnp.stack([half_of(a, which, first, heads) for a in (latent_keys, latent_values)])

    def whereabouts(*tables):
        table = jnp.concatenate(tables, axis=0)
        lists, segments = table[:, :8], table[::2, 8]

        def held(which):
            side = 2 * which - 1
            return [
                2 * x + which,
                2 * (1 - x) + which,
                2 * x + which - 4 * side,
                2 * (1 - x) + which - 4 * side,
                2 - which + 4 * side,
            ]

        offsets = jnp.stack(held(core) + held(1 - core))
        wanted = lists // 2 - 4 * row
        position = jnp.argmax(wanted[:, :, None] == offsets[None, None, :], axis=2).astype(jnp.int32)
        valid = (lists >= 0).astype(jnp.int32)
        slots = jnp.where(lists >= 0, position * 2 + lists % 2, 0)
        ahead = 2 * segments[:, None] + jnp.arange(2)[None, :] - z
        text_at = jnp.where(row % YN < 2, -ahead, ahead) % ZN
        return (x[None].astype(jnp.int32), slots, valid, text_at.astype(jnp.int32))

    firsts = [sum(CHUNKS[:i]) for i in range(len(CHUNKS))]
    give1 = pair_of(1 - x, firsts[0], CHUNKS[0])
    kv_own = pair_of(x)

    own_table = jnp.concatenate(
        [block_lists, jnp.broadcast_to(tile_segment[:, None], (2, 8))], axis=1
    )
    far_table = send("table", own_table, ACROSS)
    halves = jnp.stack([prompt_keyvals[..., :width], prompt_keyvals[..., width:]])
    spread = jnp.broadcast_to(halves[None], (YN, *halves.shape))
    plane = lax.all_to_all(
        spread.reshape(YN * XN, *halves.shape[1:]), "seq", 0, 0, axis_index_groups=PLANES
    )
    plane = jnp.swapaxes(plane, 0, 1).reshape(2, 64, width)
    far1 = send("far", give1, ACROSS)
    kv_own, plane, far_table, queries, latent_keys, latent_values = lax.optimization_barrier(
        (kv_own, plane, far_table, queries, latent_keys, latent_values)
    )
    scalars = whereabouts(own_table, far_table)
    out_own = send("out_own", kv_own, OUTWARD)
    hop1 = send("text_z", plane, MAJOR)
    give2, q_give, hop1, far1, out_own, kv_own, *scalars = lax.optimization_barrier(
        (
            pair_of(1 - x, firsts[1], CHUNKS[1]), half_of(queries, 1 - x),
            hop1, far1, out_own, kv_own, *scalars,
        )
    )

    def between(first, heads, far):
        return jnp.where(x != core, kv_own[..., first * HD : (first + heads) * HD], far)

    def swapped(i, far, out_far, mid):
        held_here = gather_heads(firsts[i], CHUNKS[i], kv_own, far, out_own, out_far, mid)
        return send("cc_part", held_here, CORES)

    def attended(i, far, out_far, mid, cc_part):
        return latent(
            firsts[i], CHUNKS[i], scalars, queries, q_far, latent_keys, latent_values,
            far, out_own, out_far, mid, cc_part,
        )

    far2 = send("far", give2, ACROSS)
    q_far = send("q_far", q_give, ACROSS)
    out_far1 = send("out_far", far1, OUTWARD)
    mid1 = send("mid", between(firsts[0], CHUNKS[0], far1), INWARD)
    hop2 = send("text_z", hop1, MAJOR)
    hop3 = send("text_z", hop2, MAJOR)
    far2, q_far, out_far1, mid1, hop3 = lax.optimization_barrier(
        (far2, q_far, out_far1, mid1, hop3)
    )

    out_far2 = send("out_far", far2, OUTWARD)
    mid2 = send("mid", between(firsts[1], CHUNKS[1], far2), INWARD)
    hop4 = send("text_z", hop3, MAJOR)
    hop5 = send("text_z", hop4, MAJOR)
    sums1 = attended(0, far1, out_far1, mid1, swapped(0, far1, out_far1, mid1))
    out_far2, mid2, hop5, plane, *sums1 = lax.optimization_barrier(
        (out_far2, mid2, hop5, plane, *sums1)
    )

    hop6, other = send("text_z", hop5, MAJOR), send("text_z", plane, MINOR)
    near = pack(plane, hop1, hop2, hop3, hop4, hop5)
    cc_near = send("cc_text", near, CORES)
    sums2 = attended(1, far2, out_far2, mid2, swapped(1, far2, out_far2, mid2))
    hop6, other, _, _ = lax.optimization_barrier((hop6, other, *sums2))
    last = pack(hop6, other)
    cc_last = send("cc_text", last, CORES)
    text = (near, last, cc_near, cc_last)
    results = []
    for first, heads, sums in zip(firsts, CHUNKS, (sums1, sums2)):
        mine, theirs = finish(first, heads, scalars, queries, q_far, *sums, *text)
        results.append((mine, send("back", theirs, ACROSS)))
    mine = jnp.concatenate([m for m, _ in results], axis=1)
    back = jnp.concatenate([b for _, b in results], axis=1)
    left, right = jnp.where(x == 0, mine, back), jnp.where(x == 0, back, mine)
    return jnp.concatenate([left, right], axis=1)


def solution(mesh):
    in_specs = (
        P(("cfg", "seq"), None),
        P(("cfg", "seq"), None),
        P(("cfg", "seq"), None),
        P(None, ("cfg", "seq"), None),
        P("seq", None),
        P("seq"),
    )
    out_specs = P(("cfg", "seq"), None)
    return jax.shard_map(
        on_device, mesh=mesh, in_specs=in_specs, out_specs=out_specs, check_vma=False
    )
```

```python
import functools
import math

import jax
import jax.numpy as jnp
from jax import lax
from jax.experimental import pallas as pl
from jax.experimental.pallas import tpu as pltpu
from jax.sharding import PartitionSpec as P

HD = 128
BLK = 128
TOK = 256
ZN, YN, XN, CN = 8, 4, 2, 2
ROWS = ZN * YN
HALF = 10
CHUNKS = (6, 4)
NEG = -1e30
C2 = math.log2(math.e) / math.sqrt(HD)


def place(row, x, core):
    return ((row % ROWS) * XN + x % XN) * CN + core % CN


DEVICES = [(r, x, c) for r in range(ROWS) for x in range(XN) for c in range(CN)]


def route(to):
    return [(place(*d), place(*to(*d))) for d in DEVICES]


ACROSS = route(lambda r, x, c: (r, 1 - x, c))
CORES = route(lambda r, x, c: (r, x, 1 - c))
OUTWARD = route(lambda r, x, c: (r + (1 if c else -1), x, c))
INWARD = route(lambda r, x, c: (r + (-1 if c else 1), x, c))
MAJOR = route(lambda r, x, c: (r + (YN if r % YN < 2 else -YN), x, c))
MINOR = route(lambda r, x, c: (r - (YN if r % YN < 2 else -YN), x, c))


def pack_kernel(*refs):
    whole = refs[-1]
    for i, block in enumerate(refs[:-1]):

        @pl.when(pl.program_id(0) == i)
        def _():
            whole[...] = block[...]


def pack(*blocks):
    shape = blocks[0].shape
    zeros = (0,) * len(shape)
    return pl.pallas_call(
        pack_kernel,
        out_shape=jax.ShapeDtypeStruct((len(blocks), *shape), blocks[0].dtype),
        grid=(len(blocks),),
        in_specs=[pl.BlockSpec(shape, lambda i: zeros)] * len(blocks),
        out_specs=pl.BlockSpec((None, *shape), lambda i: (i, *zeros)),
        compiler_params=pltpu.CompilerParams(vmem_limit_bytes=32 * 1024 * 1024),
        name="pack",
    )(*blocks)


def gather_kernel(*refs):
    whole = refs[-1]
    for i, pair in enumerate(refs[:-1]):
        whole[i] = pair[...]


def gather_heads(first, heads, *pairs):
    pair = (2, TOK, HD)

    def spec(width):
        start = first if width == HALF * HD else 0
        return pl.BlockSpec(pair, lambda i: (0, 0, start + i))

    return pl.pallas_call(
        gather_kernel,
        out_shape=jax.ShapeDtypeStruct((len(pairs), 2, TOK, heads * HD), jnp.bfloat16),
        grid=(heads,),
        in_specs=[spec(p.shape[-1]) for p in pairs],
        out_specs=pl.BlockSpec((len(pairs), *pair), lambda i: (0, 0, 0, i)),
        compiler_params=pltpu.CompilerParams(vmem_limit_bytes=32 * 1024 * 1024),
        name="gather_heads",
    )(*pairs)


def softened(parts, top):
    weights = [jnp.exp2((part - top) * C2) for part in parts]
    total = jnp.sum(functools.reduce(jnp.add, weights), axis=1, keepdims=True)
    return jnp.concatenate([w.astype(jnp.bfloat16) for w in weights], axis=1), total


def scored(query, keys):
    return lax.dot_general(query, keys, (((1,), (1,)), ((), ())), preferred_element_type=jnp.float32)


GROUP = 2
UNITS = [
    (tile, slice(block * BLK, (block + 1) * BLK), tile * 2 + block)
    for tile in range(2)
    for block in range(TOK // BLK)
]


def latent_kernel(
    half_ref, slots_ref, valid_ref, text_at_ref,
    q_own, q_far, k_own, v_own, far, out_own, out_far, mid, cc_part,
    sums, tops, totals, keys, values,
):
    tiles = [
        (k_own, v_own),
        *[(pair.at[0], pair.at[1]) for pair in (far, out_own, out_far, mid)],
        *[(cc_part.at[i, 0], cc_part.at[i, 1]) for i in range(5)],
    ]
    for at, (k, v) in enumerate(tiles):
        keys[at * TOK : (at + 1) * TOK, :] = k[...]
        values[at * TOK : (at + 1) * TOK, :] = v[...]

    def listed(row, store):
        starts = [pl.multiple_of(slots_ref[row, s] * BLK, BLK) for s in range(8)]
        return jnp.concatenate([store[pl.ds(at, BLK), :] for at in starts], axis=0)

    def score(unit):
        tile, rows, row = unit
        scores = scored((q_own, q_far)[tile][rows, :], listed(row, keys))
        parts = [scores[:, s * BLK : (s + 1) * BLK] for s in range(8)]
        for s in range(1, 8):
            parts[s] = jnp.where(valid_ref[row, s] > 0, parts[s], NEG)
        return parts

    ahead = score(UNITS[0])
    for unit, later in zip(UNITS, UNITS[1:] + [None]):
        parts, ahead = ahead, score(later) if later else None
        tile, rows, row = unit
        top = jnp.max(functools.reduce(jnp.maximum, parts), axis=1, keepdims=True)
        rounded, total = softened(parts, top)
        sums[tile, rows, :] = jnp.dot(
            rounded, listed(row, values), preferred_element_type=jnp.float32
        )
        tops[tile, rows, :] = jnp.broadcast_to(top, (BLK, HD))
        totals[tile, rows, :] = jnp.broadcast_to(total, (BLK, HD))


def text_kernel(
    half_ref, slots_ref, valid_ref, text_at_ref,
    q_own, q_far, sums, tops, totals, near, last, cc_near, cc_last, o_own, o_far, keys, values,
):
    for core, (most, other) in enumerate(((near, last), (cc_near, cc_last))):
        planes = [most.at[i] for i in range(6)] + [other.at[i] for i in range(2)]
        for at, plane in enumerate(planes):
            to = at * BLK + core * 64
            keys[to : to + 64, :] = plane[0]
            values[to : to + 64, :] = plane[1]

    units = [
        (tile, rows, slice(head * HD, (head + 1) * HD))
        for head in range(GROUP)
        for tile, rows, _ in UNITS
    ]

    def listed(unit, store):
        tile, _, cols = unit
        starts = [pl.multiple_of(text_at_ref[tile, i] * BLK, BLK) for i in range(2)]
        return jnp.concatenate([store[pl.ds(at, BLK), cols] for at in starts], axis=0)

    scores = [
        scored((q_own, q_far)[unit[0]][unit[1], unit[2]], listed(unit, keys)) for unit in units
    ]
    parts = [[score[:, :BLK], score[:, BLK:]] for score in scores]
    highest = [
        jnp.maximum(tops[unit], jnp.max(jnp.maximum(*part), axis=1, keepdims=True))
        for unit, part in zip(units, parts)
    ]
    softs = [softened(part, top) for part, top in zip(parts, highest)]
    mixes = [
        jnp.dot(rounded, listed(unit, values), preferred_element_type=jnp.float32)
        for (rounded, _), unit in zip(softs, units)
    ]
    for unit, top, (_, total), mixed in zip(units, highest, softs, mixes):
        fade = jnp.exp2((tops[unit] - top) * C2)
        mixed = (sums[unit] * fade + mixed) / (totals[unit] * fade + total)
        (o_own, o_far)[unit[0]][unit[1], unit[2]] = mixed.astype(jnp.bfloat16)


def specs_of(first, group=1):
    def whole(i, half, *_):
        return (0, half[0] * (HALF // group) + first // group + i)

    def halved(lead):
        return lambda i, *_: (0,) * lead + (first // group + i,)

    def chunk(lead):
        return lambda i, *_: (0,) * lead + (i,)

    return whole, halved, chunk


def call(kernel, name, heads, keys, in_specs, out_shape, out_specs, scratch, arguments):
    return pl.pallas_call(
        kernel,
        out_shape=out_shape,
        grid_spec=pltpu.PrefetchScalarGridSpec(
            num_scalar_prefetch=4,
            grid=(heads * HD // scratch[1],),
            in_specs=in_specs,
            out_specs=out_specs,
            scratch_shapes=[pltpu.VMEM(scratch, jnp.bfloat16)] * 2,
        ),
        compiler_params=pltpu.CompilerParams(vmem_limit_bytes=56 * 1024 * 1024),
        cost_estimate=pl.CostEstimate(
            flops=heads * 4 * BLK * keys * HD * 4 * 6,
            bytes_accessed=heads * keys * 2000,
            transcendentals=heads * 4 * BLK * keys,
        ),
        name=name,
    )(*arguments)


def latent(first, heads, scalars, *arrays):
    whole, halved, chunk = specs_of(first)
    pair = (2, TOK, HD)
    in_specs = [
        pl.BlockSpec((TOK, HD), whole),
        pl.BlockSpec((TOK, HD), halved(1)),
        pl.BlockSpec((TOK, HD), whole),
        pl.BlockSpec((TOK, HD), whole),
        pl.BlockSpec(pair, chunk(2)),
        pl.BlockSpec(pair, halved(2)),
        pl.BlockSpec(pair, chunk(2)),
        pl.BlockSpec(pair, chunk(2)),
        pl.BlockSpec((5, *pair), chunk(3)),
    ]
    out = jax.ShapeDtypeStruct((2, TOK, heads * HD), jnp.float32)
    out_specs = (pl.BlockSpec(pair, chunk(2)),) * 3
    return call(
        latent_kernel, "latent", heads, 1024, in_specs, (out,) * 3, out_specs, (10 * TOK, HD),
        (*scalars, *arrays),
    )


def finish(first, heads, scalars, *arrays):
    whole, halved, chunk = specs_of(first, GROUP)
    wide = GROUP * HD
    in_specs = [
        pl.BlockSpec((TOK, wide), whole),
        pl.BlockSpec((TOK, wide), halved(1)),
        *[pl.BlockSpec((2, TOK, wide), chunk(2))] * 3,
        *[pl.BlockSpec((n, 2, 64, wide), halved(3)) for n in (6, 2, 6, 2)],
    ]
    out = jax.ShapeDtypeStruct((TOK, heads * HD), jnp.bfloat16)
    out_specs = (pl.BlockSpec((TOK, wide), chunk(1)),) * 2
    return call(
        text_kernel, "finish", heads, 256, in_specs, (out, out), out_specs, (ZN * BLK, wide),
        (*scalars, *arrays),
    )


PLANES = [
    [place(z * YN + y, x, c) for y in range(YN) for x in range(XN)]
    for z in range(ZN)
    for c in range(CN)
]


def send(what, block, to):
    with jax.named_scope(what):
        return lax.ppermute(block, "seq", to)


def on_device(queries, latent_keys, latent_values, prompt_keyvals, block_lists, tile_segment):
    width = HALF * HD
    device = lax.axis_index("seq")
    core, x, row = device % CN, device // CN % XN, device // (CN * XN)
    z = row // YN

    def half_of(array, which, first=0, heads=HALF):
        start = which * width + first * HD
        return lax.dynamic_slice_in_dim(array, start, heads * HD, array.ndim - 1)

    def pair_of(which, first=0, heads=HALF):
        return jnp.stack([half_of(a, which, first, heads) for a in (latent_keys, latent_values)])

    def whereabouts(*tables):
        table = jnp.concatenate(tables, axis=0)
        lists, segments = table[:, :8], table[::2, 8]

        def held(which):
            side = 2 * which - 1
            return [
                2 * x + which,
                2 * (1 - x) + which,
                2 * x + which - 4 * side,
                2 * (1 - x) + which - 4 * side,
                2 - which + 4 * side,
            ]

        offsets = jnp.stack(held(core) + held(1 - core))
        wanted = lists // 2 - 4 * row
        position = jnp.argmax(wanted[:, :, None] == offsets[None, None, :], axis=2).astype(jnp.int32)
        valid = (lists >= 0).astype(jnp.int32)
        slots = jnp.where(lists >= 0, position * 2 + lists % 2, 0)
        ahead = 2 * segments[:, None] + jnp.arange(2)[None, :] - z
        text_at = jnp.where(row % YN < 2, -ahead, ahead) % ZN
        return (x[None].astype(jnp.int32), slots, valid, text_at.astype(jnp.int32))

    firsts = [sum(CHUNKS[:i]) for i in range(len(CHUNKS))]
    give1 = pair_of(1 - x, firsts[0], CHUNKS[0])
    kv_own = pair_of(x)

    own_table = jnp.concatenate(
        [block_lists, jnp.broadcast_to(tile_segment[:, None], (2, 8))], axis=1
    )
    far_table = send("table", own_table, ACROSS)
    halves = jnp.stack([prompt_keyvals[..., :width], prompt_keyvals[..., width:]])
    spread = jnp.broadcast_to(halves[None], (YN, *halves.shape))
    plane = lax.all_to_all(
        spread.reshape(YN * XN, *halves.shape[1:]), "seq", 0, 0, axis_index_groups=PLANES
    )
    plane = jnp.swapaxes(plane, 0, 1).reshape(2, 64, width)
    far1 = send("far", give1, ACROSS)
    kv_own, plane, far_table, queries, latent_keys, latent_values = lax.optimization_barrier(
        (kv_own, plane, far_table, queries, latent_keys, latent_values)
    )
    scalars = whereabouts(own_table, far_table)
    out_own = send("out_own", kv_own, OUTWARD)
    hop1 = send("text_z", plane, MAJOR)
    give2, q_give, hop1, far1, out_own, kv_own, *scalars = lax.optimization_barrier(
        (
            pair_of(1 - x, firsts[1], CHUNKS[1]), half_of(queries, 1 - x),
            hop1, far1, out_own, kv_own, *scalars,
        )
    )

    def between(first, heads, far):
        return jnp.where(x != core, kv_own[..., first * HD : (first + heads) * HD], far)

    def swapped(i, far, out_far, mid):
        held_here = gather_heads(firsts[i], CHUNKS[i], kv_own, far, out_own, out_far, mid)
        return send("cc_part", held_here, CORES)

    def attended(i, far, out_far, mid, cc_part):
        return latent(
            firsts[i], CHUNKS[i], scalars, queries, q_far, latent_keys, latent_values,
            far, out_own, out_far, mid, cc_part,
        )

    far2 = send("far", give2, ACROSS)
    q_far = send("q_far", q_give, ACROSS)
    out_far1 = send("out_far", far1, OUTWARD)
    mid1 = send("mid", between(firsts[0], CHUNKS[0], far1), INWARD)
    hop2 = send("text_z", hop1, MAJOR)
    hop3 = send("text_z", hop2, MAJOR)
    far2, q_far, out_far1, mid1, hop3 = lax.optimization_barrier(
        (far2, q_far, out_far1, mid1, hop3)
    )

    out_far2 = send("out_far", far2, OUTWARD)
    mid2 = send("mid", between(firsts[1], CHUNKS[1], far2), INWARD)
    hop4 = send("text_z", hop3, MAJOR)
    hop5 = send("text_z", hop4, MAJOR)
    sums1 = attended(0, far1, out_far1, mid1, swapped(0, far1, out_far1, mid1))
    out_far2, mid2, hop5, plane, *sums1 = lax.optimization_barrier(
        (out_far2, mid2, hop5, plane, *sums1)
    )

    hop6, other = send("text_z", hop5, MAJOR), send("text_z", plane, MINOR)
    near = pack(plane, hop1, hop2, hop3, hop4, hop5)
    cc_near = send("cc_text", near, CORES)
    sums2 = attended(1, far2, out_far2, mid2, swapped(1, far2, out_far2, mid2))
    hop6, other, *_ = lax.optimization_barrier((hop6, other, *sums2))
    last = pack(hop6, other)
    cc_last = send("cc_text", last, CORES)
    text = (near, last, cc_near, cc_last)
    results = []
    for first, heads, sums in zip(firsts, CHUNKS, (sums1, sums2)):
        mine, theirs = finish(first, heads, scalars, queries, q_far, *sums, *text)
        results.append((mine, send("back", theirs, ACROSS)))
    mine = jnp.concatenate([m for m, _ in results], axis=1)
    back = jnp.concatenate([b for _, b in results], axis=1)
    left, right = jnp.where(x == 0, mine, back), jnp.where(x == 0, back, mine)
    return jnp.concatenate([left, right], axis=1)


def solution(mesh):
    in_specs = (
        P(("cfg", "seq"), None),
        P(("cfg", "seq"), None),
        P(("cfg", "seq"), None),
        P(None, ("cfg", "seq"), None),
        P("seq", None),
        P("seq"),
    )
    out_specs = P(("cfg", "seq"), None)
    return jax.shard_map(
        on_device, mesh=mesh, in_specs=in_specs, out_specs=out_specs, check_vma=False
    )
```

```python
import functools
import math

import jax
import jax.numpy as jnp
from jax import lax
from jax.experimental import pallas as pl
from jax.experimental.pallas import tpu as pltpu
from jax.sharding import PartitionSpec as P

HD = 128
BLK = 128
TOK = 256
ZN, YN, XN, CN = 8, 4, 2, 2
ROWS = ZN * YN
HALF = 10
CHUNKS = (6, 4)
NEG = -1e30
C2 = math.log2(math.e) / math.sqrt(HD)


def place(row, x, core):
    return ((row % ROWS) * XN + x % XN) * CN + core % CN


DEVICES = [(r, x, c) for r in range(ROWS) for x in range(XN) for c in range(CN)]


def route(to):
    return [(place(*d), place(*to(*d))) for d in DEVICES]


ACROSS = route(lambda r, x, c: (r, 1 - x, c))
CORES = route(lambda r, x, c: (r, x, 1 - c))
OUTWARD = route(lambda r, x, c: (r + (1 if c else -1), x, c))
INWARD = route(lambda r, x, c: (r + (-1 if c else 1), x, c))
MAJOR = route(lambda r, x, c: (r + (YN if r % YN < 2 else -YN), x, c))
MINOR = route(lambda r, x, c: (r - (YN if r % YN < 2 else -YN), x, c))


def pack_kernel(*refs):
    whole = refs[-1]
    for i, block in enumerate(refs[:-1]):

        @pl.when(pl.program_id(0) == i)
        def _():
            whole[...] = block[...]


def pack(*blocks):
    shape = blocks[0].shape
    zeros = (0,) * len(shape)
    return pl.pallas_call(
        pack_kernel,
        out_shape=jax.ShapeDtypeStruct((len(blocks), *shape), blocks[0].dtype),
        grid=(len(blocks),),
        in_specs=[pl.BlockSpec(shape, lambda i: zeros)] * len(blocks),
        out_specs=pl.BlockSpec((None, *shape), lambda i: (i, *zeros)),
        compiler_params=pltpu.CompilerParams(vmem_limit_bytes=32 * 1024 * 1024),
        name="pack",
    )(*blocks)


def gather_kernel(*refs):
    whole = refs[-1]
    for i, pair in enumerate(refs[:-1]):
        whole[i] = pair[...]


def gather_heads(first, heads, *pairs):
    pair = (2, TOK, HD)

    def spec(width):
        start = first if width == HALF * HD else 0
        return pl.BlockSpec(pair, lambda i: (0, 0, start + i))

    return pl.pallas_call(
        gather_kernel,
        out_shape=jax.ShapeDtypeStruct((len(pairs), 2, TOK, heads * HD), jnp.bfloat16),
        grid=(heads,),
        in_specs=[spec(p.shape[-1]) for p in pairs],
        out_specs=pl.BlockSpec((len(pairs), *pair), lambda i: (0, 0, 0, i)),
        compiler_params=pltpu.CompilerParams(vmem_limit_bytes=32 * 1024 * 1024),
        name="gather_heads",
    )(*pairs)


def softened(parts, top):
    weights = [jnp.exp2((part - top) * C2) for part in parts]
    total = jnp.sum(functools.reduce(jnp.add, weights), axis=1, keepdims=True)
    return jnp.concatenate([w.astype(jnp.bfloat16) for w in weights], axis=1), total


def scored(query, keys):
    return lax.dot_general(query, keys, (((1,), (1,)), ((), ())), preferred_element_type=jnp.float32)


GROUP = 2
UNITS = [
    (tile, slice(block * BLK, (block + 1) * BLK), tile * 2 + block)
    for tile in range(2)
    for block in range(TOK // BLK)
]


def latent_kernel(
    half_ref, slots_ref, valid_ref, text_at_ref,
    q_own, q_far, k_own, v_own, far, out_own, out_far, mid, cc_part,
    sums, tops, totals, keys, values,
):
    tiles = [
        (k_own, v_own),
        *[(pair.at[0], pair.at[1]) for pair in (far, out_own, out_far, mid)],
        *[(cc_part.at[i, 0], cc_part.at[i, 1]) for i in range(5)],
    ]
    for at, (k, v) in enumerate(tiles):
        keys[at * TOK : (at + 1) * TOK, :] = k[...]
        values[at * TOK : (at + 1) * TOK, :] = v[...]

    def listed(row, store):
        starts = [pl.multiple_of(slots_ref[row, s] * BLK, BLK) for s in range(8)]
        return jnp.concatenate([store[pl.ds(at, BLK), :] for at in starts], axis=0)

    def score(unit):
        tile, rows, row = unit
        scores = scored((q_own, q_far)[tile][rows, :], listed(row, keys))
        parts = [scores[:, s * BLK : (s + 1) * BLK] for s in range(8)]
        for s in range(1, 8):
            parts[s] = jnp.where(valid_ref[row, s] > 0, parts[s], NEG)
        return parts

    ahead = score(UNITS[0])
    for unit, later in zip(UNITS, UNITS[1:] + [None]):
        parts, ahead = ahead, score(later) if later else None
        tile, rows, row = unit
        top = jnp.max(functools.reduce(jnp.maximum, parts), axis=1, keepdims=True)
        rounded, total = softened(parts, top)
        sums[tile, rows, :] = jnp.dot(
            rounded, listed(row, values), preferred_element_type=jnp.float32
        )
        tops[tile, rows, :] = jnp.broadcast_to(top, (BLK, HD))
        totals[tile, rows, :] = jnp.broadcast_to(total, (BLK, HD))


def text_kernel(
    half_ref, slots_ref, valid_ref, text_at_ref,
    q_own, q_far, sums, tops, totals, near, last, cc_near, cc_last, o_own, o_far, keys, values,
):
    for core, (most, other) in enumerate(((near, last), (cc_near, cc_last))):
        planes = [most.at[i] for i in range(6)] + [other.at[i] for i in range(2)]
        for at, plane in enumerate(planes):
            to = at * BLK + core * 64
            keys[to : to + 64, :] = plane[0]
            values[to : to + 64, :] = plane[1]

    units = [
        (tile, rows, slice(head * HD, (head + 1) * HD))
        for head in range(GROUP)
        for tile, rows, _ in UNITS
    ]

    def listed(unit, store):
        tile, _, cols = unit
        starts = [pl.multiple_of(text_at_ref[tile, i] * BLK, BLK) for i in range(2)]
        return jnp.concatenate([store[pl.ds(at, BLK), cols] for at in starts], axis=0)

    scores = [
        scored((q_own, q_far)[unit[0]][unit[1], unit[2]], listed(unit, keys)) for unit in units
    ]
    parts = [[score[:, :BLK], score[:, BLK:]] for score in scores]
    highest = [
        jnp.maximum(tops[unit], jnp.max(jnp.maximum(*part), axis=1, keepdims=True))
        for unit, part in zip(units, parts)
    ]
    softs = [softened(part, top) for part, top in zip(parts, highest)]
    mixes = [
        jnp.dot(rounded, listed(unit, values), preferred_element_type=jnp.float32)
        for (rounded, _), unit in zip(softs, units)
    ]
    for unit, top, (_, total), mixed in zip(units, highest, softs, mixes):
        fade = jnp.exp2((tops[unit] - top) * C2)
        mixed = (sums[unit] * fade + mixed) / (totals[unit] * fade + total)
        (o_own, o_far)[unit[0]][unit[1], unit[2]] = mixed.astype(jnp.bfloat16)


def specs_of(first, group=1):
    def whole(i, half, *_):
        return (0, half[0] * (HALF // group) + first // group + i)

    def halved(lead):
        return lambda i, *_: (0,) * lead + (first // group + i,)

    def chunk(lead):
        return lambda i, *_: (0,) * lead + (i,)

    return whole, halved, chunk


def call(kernel, name, heads, keys, in_specs, out_shape, out_specs, scratch, arguments):
    return pl.pallas_call(
        kernel,
        out_shape=out_shape,
        grid_spec=pltpu.PrefetchScalarGridSpec(
            num_scalar_prefetch=4,
            grid=(heads * HD // scratch[1],),
            in_specs=in_specs,
            out_specs=out_specs,
            scratch_shapes=[pltpu.VMEM(scratch, jnp.bfloat16)] * 2,
        ),
        compiler_params=pltpu.CompilerParams(vmem_limit_bytes=56 * 1024 * 1024),
        cost_estimate=pl.CostEstimate(
            flops=heads * 4 * BLK * keys * HD * 4 * 6,
            bytes_accessed=heads * keys * 2000,
            transcendentals=heads * 4 * BLK * keys,
        ),
        name=name,
    )(*arguments)


def latent(first, heads, scalars, *arrays):
    whole, halved, chunk = specs_of(first)
    pair = (2, TOK, HD)
    in_specs = [
        pl.BlockSpec((TOK, HD), whole),
        pl.BlockSpec((TOK, HD), halved(1)),
        pl.BlockSpec((TOK, HD), whole),
        pl.BlockSpec((TOK, HD), whole),
        pl.BlockSpec(pair, chunk(2)),
        pl.BlockSpec(pair, halved(2)),
        pl.BlockSpec(pair, chunk(2)),
        pl.BlockSpec(pair, chunk(2)),
        pl.BlockSpec((5, *pair), chunk(3)),
    ]
    out = jax.ShapeDtypeStruct((2, TOK, heads * HD), jnp.float32)
    out_specs = (pl.BlockSpec(pair, chunk(2)),) * 3
    return call(
        latent_kernel, "latent", heads, 1024, in_specs, (out,) * 3, out_specs, (10 * TOK, HD),
        (*scalars, *arrays),
    )


def finish(first, heads, scalars, *arrays):
    whole, halved, chunk = specs_of(first, GROUP)
    wide = GROUP * HD
    in_specs = [
        pl.BlockSpec((TOK, wide), whole),
        pl.BlockSpec((TOK, wide), halved(1)),
        *[pl.BlockSpec((2, TOK, wide), chunk(2))] * 3,
        *[pl.BlockSpec((n, 2, 64, wide), halved(3)) for n in (6, 2, 6, 2)],
    ]
    out = jax.ShapeDtypeStruct((TOK, heads * HD), jnp.bfloat16)
    out_specs = (pl.BlockSpec((TOK, wide), chunk(1)),) * 2
    return call(
        text_kernel, "finish", heads, 256, in_specs, (out, out), out_specs, (ZN * BLK, wide),
        (*scalars, *arrays),
    )


PLANES = [
    [place(z * YN + y, x, c) for y in range(YN) for x in range(XN)]
    for z in range(ZN)
    for c in range(CN)
]


def send(what, block, to):
    with jax.named_scope(what):
        return lax.ppermute(block, "seq", to)


def on_device(queries, latent_keys, latent_values, prompt_keyvals, block_lists, tile_segment):
    width = HALF * HD
    device = lax.axis_index("seq")
    core, x, row = device % CN, device // CN % XN, device // (CN * XN)
    z = row // YN

    def half_of(array, which, first=0, heads=HALF):
        start = which * width + first * HD
        return lax.dynamic_slice_in_dim(array, start, heads * HD, array.ndim - 1)

    def pair_of(which, first=0, heads=HALF):
        return jnp.stack([half_of(a, which, first, heads) for a in (latent_keys, latent_values)])

    def whereabouts(*tables):
        table = jnp.concatenate(tables, axis=0)
        lists, segments = table[:, :8], table[::2, 8]

        def held(which):
            side = 2 * which - 1
            return [
                2 * x + which,
                2 * (1 - x) + which,
                2 * x + which - 4 * side,
                2 * (1 - x) + which - 4 * side,
                2 - which + 4 * side,
            ]

        offsets = jnp.stack(held(core) + held(1 - core))
        wanted = lists // 2 - 4 * row
        position = jnp.argmax(wanted[:, :, None] == offsets[None, None, :], axis=2).astype(jnp.int32)
        valid = (lists >= 0).astype(jnp.int32)
        slots = jnp.where(lists >= 0, position * 2 + lists % 2, 0)
        ahead = 2 * segments[:, None] + jnp.arange(2)[None, :] - z
        text_at = jnp.where(row % YN < 2, -ahead, ahead) % ZN
        return (x[None].astype(jnp.int32), slots, valid, text_at.astype(jnp.int32))

    firsts = [sum(CHUNKS[:i]) for i in range(len(CHUNKS))]
    give1 = pair_of(1 - x, firsts[0], CHUNKS[0])
    kv_own = pair_of(x)

    own_table = jnp.concatenate(
        [block_lists, jnp.broadcast_to(tile_segment[:, None], (2, 8))], axis=1
    )
    far_table = send("table", own_table, ACROSS)
    halves = jnp.stack([prompt_keyvals[..., :width], prompt_keyvals[..., width:]])
    spread = jnp.broadcast_to(halves[None], (YN, *halves.shape))
    plane = lax.all_to_all(
        spread.reshape(YN * XN, *halves.shape[1:]), "seq", 0, 0, axis_index_groups=PLANES
    )
    plane = jnp.swapaxes(plane, 0, 1).reshape(2, 64, width)
    far1 = send("far", give1, ACROSS)
    kv_own, plane, far_table, queries, latent_keys, latent_values = lax.optimization_barrier(
        (kv_own, plane, far_table, queries, latent_keys, latent_values)
    )
    scalars = whereabouts(own_table, far_table)
    out_own = send("out_own", kv_own, OUTWARD)
    hop1 = send("text_z", plane, MAJOR)
    far1, q_give = lax.optimization_barrier((far1, half_of(queries, 1 - x)))
    q_far = send("q_far", q_give, ACROSS)
    give2, hop1, far1, out_own, kv_own, *scalars = lax.optimization_barrier(
        (
            pair_of(1 - x, firsts[1], CHUNKS[1]),
            hop1, far1, out_own, kv_own, *scalars,
        )
    )

    def between(first, heads, far):
        return jnp.where(x != core, kv_own[..., first * HD : (first + heads) * HD], far)

    def swapped(i, far, out_far, mid):
        held_here = gather_heads(firsts[i], CHUNKS[i], kv_own, far, out_own, out_far, mid)
        return send("cc_part", held_here, CORES)

    def attended(i, far, out_far, mid, cc_part):
        return latent(
            firsts[i], CHUNKS[i], scalars, queries, q_far, latent_keys, latent_values,
            far, out_own, out_far, mid, cc_part,
        )

    far2 = send("far", give2, ACROSS)
    out_far1 = send("out_far", far1, OUTWARD)
    mid1 = send("mid", between(firsts[0], CHUNKS[0], far1), INWARD)
    hop2 = send("text_z", hop1, MAJOR)
    hop3 = send("text_z", hop2, MAJOR)
    far2, q_far, out_far1, mid1, hop3 = lax.optimization_barrier(
        (far2, q_far, out_far1, mid1, hop3)
    )

    out_far2 = send("out_far", far2, OUTWARD)
    mid2 = send("mid", between(firsts[1], CHUNKS[1], far2), INWARD)
    hop4 = send("text_z", hop3, MAJOR)
    hop5 = send("text_z", hop4, MAJOR)
    sums1 = attended(0, far1, out_far1, mid1, swapped(0, far1, out_far1, mid1))
    out_far2, mid2, hop5, plane, *sums1 = lax.optimization_barrier(
        (out_far2, mid2, hop5, plane, *sums1)
    )

    hop6, other = send("text_z", hop5, MAJOR), send("text_z", plane, MINOR)
    near = pack(plane, hop1, hop2, hop3, hop4, hop5)
    cc_near = send("cc_text", near, CORES)
    sums2 = attended(1, far2, out_far2, mid2, swapped(1, far2, out_far2, mid2))
    hop6, other, *_ = lax.optimization_barrier((hop6, other, *sums2))
    last = pack(hop6, other)
    cc_last = send("cc_text", last, CORES)
    text = (near, last, cc_near, cc_last)
    results = []
    for first, heads, sums in zip(firsts, CHUNKS, (sums1, sums2)):
        mine, theirs = finish(first, heads, scalars, queries, q_far, *sums, *text)
        results.append((mine, send("back", theirs, ACROSS)))
    mine = jnp.concatenate([m for m, _ in results], axis=1)
    back = jnp.concatenate([b for _, b in results], axis=1)
    left, right = jnp.where(x == 0, mine, back), jnp.where(x == 0, back, mine)
    return jnp.concatenate([left, right], axis=1)


def solution(mesh):
    in_specs = (
        P(("cfg", "seq"), None),
        P(("cfg", "seq"), None),
        P(("cfg", "seq"), None),
        P(None, ("cfg", "seq"), None),
        P("seq", None),
        P("seq"),
    )
    out_specs = P(("cfg", "seq"), None)
    return jax.shard_map(
        on_device, mesh=mesh, in_specs=in_specs, out_specs=out_specs, check_vma=False
    )
```
